32 devices in a mesh: dp: 8 (over y, x, core), fsdp: 4 (over z).
Axes of the slice: x: 2, y: 2, z: 4, core: 2. Of those that a mesh axis runs over, the one named last changes fastest.
Arguments:
- layer_input: bfloat16 [4096, 8192], P(('dp', 'fsdp')), may hold values from -24 to 24
- norm_gain: float32 [8192], P('fsdp'), may hold values from 0.4 to 2.4
- value_weight: bfloat16 [8192, 512], P('fsdp'), may hold values from -0.25 to 0.25
- value_cotangent: bfloat16 [4096, 512], P(('dp', 'fsdp')), may hold values from -36 to 36
Outputs:
- input_grad: bfloat16 [4096, 8192], P(('dp', 'fsdp'))
- weight_update: bfloat16 [8192, 512], P('fsdp', 'dp')
- gain_update: bfloat16 [8192], P('fsdp')
The draws below stay inside these ranges and needn't reach their ends.
All inputs are finite; a program needn't handle non-finite values.
Results may differ from the reference program's by a relative error of at most 0.015.
Values may be sent and summed in bfloat16 or wider, within the bound.
A program may use at most 64 MiB of HBM per device.

```python
import math
import jax
import jax.numpy as jnp
import numpy as np
from jax import lax

D = 8192
W = 512
REPL_TOK = 512
TOKENS = 4096
LEVELS = 3
N_DP = 8


def shared_mix(key, width, low_end, high_end, rep_low, rep_high):
    count_repl = TOKENS // REPL_TOK
    factor = jax.random.uniform(jax.random.fold_in(key, 77), (count_repl,), jnp.float32, rep_low, rep_high)
    flipped = jax.random.bernoulli(jax.random.fold_in(key, 91 + width), 0.5, ())
    position = (jnp.arange(width).astype(jnp.float32) + 0.5) / width
    position = jnp.where(flipped, 1.0 - position, position)
    ramp = low_end + (high_end - low_end) * position
    return factor[:, None] * ramp[None, :]


def blended(key, width, low_end, high_end, rep_low, rep_high, scale_low, scale_high):
    mixing = shared_mix(key, width, low_end, high_end, rep_low, rep_high)
    key = jax.random.fold_in(key, width + 5)
    key_common, key_own, key_rows = jax.random.split(key, 3)
    common = jnp.clip(jax.random.normal(key_common, (REPL_TOK, width), jnp.float32), -4.0, 4.0)
    own = jnp.clip(jax.random.normal(key_own, (TOKENS, width), jnp.float32), -4.0, 4.0)
    replica = jnp.arange(TOKENS) // REPL_TOK
    weight_shared = mixing[replica]
    tiled = jnp.tile(common, (TOKENS // REPL_TOK, 1))
    row_scales = jnp.exp(jax.random.uniform(key_rows, (TOKENS, 1), jnp.float32, jnp.log(scale_low), jnp.log(scale_high)))
    return (row_scales * (weight_shared * tiled + jnp.sqrt(1.0 - weight_shared * weight_shared) * own), replica)


def draw_layer_input(key, part):
    low_end, high_end, rep_low, rep_high = (0.05, 0.95, 0.5, 1.0)
    values, replica = blended(key, D, low_end, high_end, rep_low, rep_high, 0.5, 4.0)
    return values.astype(jnp.bfloat16)


def draw_value_cotangent(key, part):
    low_end, high_end, rep_low, rep_high = (0.05, 0.95, 0.5, 1.0)
    values, replica = blended(key, W, low_end, high_end, rep_low, rep_high, 0.5, 2.0)
    count_repl = TOKENS // REPL_TOK
    rising = 3.0 ** (replica.astype(jnp.float32) / max(count_repl - 1, 1))
    return (values * rising[:, None]).astype(jnp.bfloat16)


def draw_norm_gain(key, part):
    key = jax.random.fold_in(key, 3)
    position = jnp.arange(D).astype(jnp.float32) / D
    base = 0.6 * 3.0 ** position
    noise = jnp.clip(1.0 + 0.12 * jax.random.normal(key, (D,), jnp.float32), 0.75, 1.25)
    return base * noise


def steps_of(key, dims, shards, smallest, high):
    level, own = 1.0, jax.random.fold_in(key, 6)
    for axis_at, parts in shards:
        heights = jnp.exp(jax.random.uniform(jax.random.fold_in(own, axis_at), (parts,), jnp.float32, smallest / len(shards), high / len(shards)))
        level = level * jnp.repeat(heights, dims[axis_at] // parts).reshape([-1 if axis == axis_at else 1 for axis in range(len(dims))])
    return level


def centred(own_key, dims, deviation, most, cuts=(), held_as=jnp.bfloat16):
    factor_of = steps_of(own_key, dims, cuts, -0.22, 0.18) if cuts else 1.0
    drawn = jax.random.normal(own_key, dims, jnp.float32) * deviation * factor_of
    return jnp.minimum(jnp.maximum(drawn, -most), most).astype(held_as)


def setup_inputs(seed: int = 0) -> dict:
    keys = jax.random.split(jax.random.key(seed), 5)
    layer_input = draw_layer_input(jax.random.fold_in(keys[4], 71), 0)
    norm_gain = draw_norm_gain(jax.random.fold_in(keys[4], 71), 0)
    value_weight = centred(keys[2], (D, W), W ** -0.5, 0.25, ((0, 4),))
    value_cotangent = draw_value_cotangent(jax.random.fold_in(keys[4], 71), 0)
    return {"layer_input": layer_input, "norm_gain": norm_gain, "value_weight": value_weight, "value_cotangent": value_cotangent}


EPS_NORM = 1e-05
EPS_SUM = 1e-06

def replica_terms(pair, norm_gain, value_weight):
    layer_input, value_cotangent = pair
    grad_scale = 1.0 / math.sqrt(REPL_TOK)
    input32 = layer_input.astype(jnp.float32)
    inverse_rms = lax.rsqrt(lax.optimization_barrier(jnp.mean(input32 * input32, axis=1, keepdims=True)) + EPS_NORM)
    normed = input32 * inverse_rms
    normed_b = lax.optimization_barrier(normed.astype(jnp.bfloat16))
    normed_bf = normed_b.astype(jnp.float32)
    scaled = (normed_bf * norm_gain[None, :]).astype(jnp.bfloat16)
    grad_w = (jnp.dot(scaled.T, value_cotangent, preferred_element_type=jnp.float32) * grad_scale).astype(jnp.bfloat16)
    back = jnp.dot(value_cotangent, value_weight.T, preferred_element_type=jnp.float32)
    grad_g = (lax.optimization_barrier(jnp.sum(back * normed_bf, axis=0)) * grad_scale).astype(jnp.bfloat16)
    hat_grad = lax.optimization_barrier((back * norm_gain[None, :]).astype(jnp.bfloat16))
    hat32 = hat_grad.astype(jnp.float32)
    mean_term = lax.optimization_barrier(jnp.mean(hat32 * normed, axis=1, keepdims=True))
    input_grad = (inverse_rms * (hat32 - normed * mean_term)).astype(jnp.bfloat16)
    return (grad_w, grad_g, input_grad)

def mix_level(vectors, pair_bit):
    partner = jnp.asarray(np.arange(N_DP) ^ 1 << pair_bit, dtype=jnp.int32)
    mine = vectors.astype(jnp.float32)
    other = jnp.take(mine, partner, axis=0)
    axes_sum = tuple(range(1, mine.ndim))
    norm_mine = lax.optimization_barrier(jnp.sum(mine * mine, axis=axes_sum))
    norm_other = lax.optimization_barrier(jnp.sum(other * other, axis=axes_sum))
    inner = lax.optimization_barrier(jnp.sum(mine * other, axis=axes_sum))
    coef_mine = 1.0 - inner / (2.0 * (norm_mine + EPS_SUM))
    coef_other = 1.0 - inner / (2.0 * (norm_other + EPS_SUM))
    shape_coef = (N_DP,) + (1,) * (mine.ndim - 1)
    return (coef_mine.reshape(shape_coef) * mine + coef_other.reshape(shape_coef) * other).astype(jnp.bfloat16)

def reference(layer_input, norm_gain, value_weight, value_cotangent):
    inputs_rep = layer_input.reshape(N_DP, REPL_TOK, D)
    cotan_rep = value_cotangent.reshape(N_DP, REPL_TOK, W)
    grad_w, grad_g, input_grad = lax.map(partial_terms(norm_gain, value_weight), (inputs_rep, cotan_rep))
    for depth_step in range(LEVELS):
        pair_bit = LEVELS - 1 - depth_step
        grad_w = mix_level(grad_w, pair_bit)
        grad_g = mix_level(grad_g, pair_bit)
    return (input_grad.reshape(TOKENS, D), grad_w[0], grad_g[0])

def partial_terms(norm_gain, value_weight):

    def apply_terms(pair):
        return replica_terms(pair, norm_gain, value_weight)
    return apply_terms
```

```python
import math

import jax
import jax.numpy as jnp
from jax import lax
from jax.sharding import PartitionSpec as P

EPS_NORM = 1e-05
EPS_SUM = 1e-06


def coefficients(gram):
    count = gram.shape[-1]
    levels = count.bit_length() - 1
    eye = jnp.eye(count, dtype=jnp.float32)
    coef = jnp.broadcast_to(eye, gram.shape)
    for depth_step in range(levels):
        stride = 1 << (levels - 1 - depth_step)

        def swap(block, axis):
            shape = block.shape
            split = shape[:axis] + (count // (2 * stride), 2, stride) + shape[axis + 1 :]
            return jnp.flip(block.reshape(split), axis + 1).reshape(shape)

        norm = jnp.maximum(jnp.sum(gram * eye, axis=-1), 0.0)
        inner = jnp.sum(gram * swap(eye, 0), axis=-1)
        mine = 1.0 - inner / (2.0 * (norm + EPS_SUM))
        other = swap(mine, 1)
        coef = mine[..., None] * coef + other[..., None] * swap(coef, 1)
        gram = mine[..., None] * gram + other[..., None] * swap(gram, 1)
        gram = mine[..., None, :] * gram + other[..., None, :] * swap(gram, 2)
    return coef[..., 0, :]


def body(layer_input, norm_gain, value_weight, value_cotangent):
    input32 = layer_input.astype(jnp.float32)
    inverse_rms = lax.rsqrt(jnp.mean(input32 * input32, axis=1, keepdims=True) + EPS_NORM)
    normed = input32 * inverse_rms
    normed_b = normed.astype(jnp.bfloat16)
    columns = lax.all_to_all(normed_b, "fsdp", split_axis=1, concat_axis=0, tiled=True)
    cotangent = lax.all_gather(value_cotangent, "fsdp", axis=0, tiled=True)
    grad_scale = 1.0 / math.sqrt(cotangent.shape[0])
    columns32 = columns.astype(jnp.float32)
    scaled = (columns32 * norm_gain[None, :]).astype(jnp.bfloat16)
    grad_w = (
        lax.dot_general(
            cotangent, scaled, (((0,), (0,)), ((), ())), preferred_element_type=jnp.float32
        )
        * grad_scale
    ).astype(jnp.bfloat16)
    back = lax.dot_general(
        cotangent, value_weight, (((1,), (1,)), ((), ())), preferred_element_type=jnp.float32
    )
    grad_g = (jnp.sum(back * columns32, axis=0) * grad_scale).astype(jnp.bfloat16)
    hat_grad = (back * norm_gain[None, :]).astype(jnp.bfloat16)
    returned = lax.all_to_all(hat_grad, "fsdp", split_axis=0, concat_axis=1, tiled=True)
    hat32 = returned.astype(jnp.float32)
    mean_term = jnp.mean(hat32 * normed, axis=1, keepdims=True)
    input_grad = (inverse_rms * (hat32 - normed * mean_term)).astype(jnp.bfloat16)
    count = lax.axis_size("dp")
    own = grad_w.shape[0] // count
    slabs = lax.all_to_all(grad_w, "dp", split_axis=0, concat_axis=0, tiled=True)
    all_g = lax.all_gather(grad_g, "dp", axis=0).astype(jnp.float32)
    products = lax.dot_general(slabs, slabs, (((1,), (1,)), ((), ())), preferred_element_type=jnp.float32)
    products = products.reshape(count, own, count, own)
    gram_w = jnp.sum(products * jnp.eye(own, dtype=jnp.float32)[None, :, None, :], axis=(1, 3))
    gram_g = jnp.sum(all_g[:, None, :] * all_g[None, :, :], axis=2) / count
    coef = coefficients(lax.psum(jnp.stack([gram_w, gram_g]), ("dp", "fsdp")))
    slabs32 = slabs.reshape(count, own, -1).astype(jnp.float32)
    weight = jnp.sum(coef[0][:, None, None] * slabs32, axis=0).astype(jnp.bfloat16)
    gain = jnp.sum(coef[1][:, None] * all_g, axis=0).astype(jnp.bfloat16)
    return (input_grad, weight.T, gain)


def solution(mesh):
    in_specs = (P(("dp", "fsdp"), None), P("fsdp"), P("fsdp", None), P(("dp", "fsdp"), None))
    out_specs = (P(("dp", "fsdp"), None), P("fsdp", "dp"), P("fsdp"))
    return jax.shard_map(body, mesh=mesh, in_specs=in_specs, out_specs=out_specs, check_vma=False)
```

```python
import functools
import math

import jax
import jax.numpy as jnp
from jax import lax
from jax.experimental import pallas as pl
from jax.experimental.pallas import tpu as pltpu
from jax.sharding import PartitionSpec as P

EPS_NORM = 1e-05
EPS_SUM = 1e-06
MESH = pl.DeviceIdType.MESH
F32 = jnp.float32
BF16 = jnp.bfloat16


def dot_t(a, b):
    return lax.dot_general(a, b, (((1,), (1,)), ((), ())), preferred_element_type=F32)


def coefficients(gram):
    count, lanes = gram.shape
    row = lax.broadcasted_iota(jnp.int32, gram.shape, 0)
    lane = lax.broadcasted_iota(jnp.int32, gram.shape, 1)
    coef = jnp.where(row == lane, 1.0, 0.0).astype(F32)
    stride = count // 2
    while stride:
        row_set = lax.rem(row // stride, 2) == 1
        lane_set = lax.rem(lane // stride, 2) == 1
        row_partner = jnp.where(row_set, row - stride, row + stride)

        def swap_rows(block):
            down = pltpu.roll(block, stride, 0)
            up = pltpu.roll(block, count - stride, 0)
            return jnp.where(row_set, down, up)

        def swap_lanes(block):
            down = pltpu.roll(block, stride, 1)
            up = pltpu.roll(block, lanes - stride, 1)
            return jnp.where(lane_set, down, up)

        own = jnp.where(row == lane, gram, 0.0)
        meet = jnp.where(row_partner == lane, gram, 0.0)

        def weights(axis):
            norm = jnp.maximum(jnp.sum(own, axis=axis, keepdims=True), 0.0)
            inner = jnp.sum(meet, axis=axis, keepdims=True)
            return jnp.broadcast_to(1.0 - inner / (2.0 * (norm + EPS_SUM)), gram.shape)

        mine, mine_lane = weights(1), weights(0)
        other, other_lane = swap_rows(mine), swap_lanes(mine_lane)
        coef = mine * coef + other * swap_rows(coef)
        gram = mine * gram + other * swap_rows(gram)
        gram = mine_lane * gram + other_lane * swap_lanes(gram)
        stride //= 2
    return coef


def kernel(
    n_d, n_f, n_k,
    x_ref, gain_ref, w_ref, cot_ref,
    ig_ref, wu_ref, gu_ref,
    inv, nb, cols, cot_all, gain_all, wall, gsend, slabs, products, g_own, g_all, gram1, gram2,
    w_send, w_recv, c_send, c_recv, n_send, n_recv, col_send, col_recv, hyp_send, hyp_recv,
    slab_send, slab_recv, g_send, g_recv, one_send, one_recv, two_send, two_recv,
):
    d, f = lax.axis_index("dp"), lax.axis_index("fsdp")
    tok, model = x_ref.shape
    owned, width = w_ref.shape
    chunk = owned // n_k
    rows = owned // n_d
    slab = width // n_d
    scale = 1.0 / math.sqrt(n_f * tok)
    sent = []

    def f_peer(o):
        return (d, lax.rem(f + o, n_f))

    def d_peer(o):
        return (lax.rem(d + o, n_d), f)

    def send(src, dst, send_sem, recv_sem, device):
        copy = pltpu.make_async_remote_copy(
            src_ref=src, dst_ref=dst, send_sem=send_sem, recv_sem=recv_sem,
            device_id=device, device_id_type=MESH,
        )
        copy.start()
        sent.append(copy)
        return copy

    def features(o, k):
        return pl.ds(pl.multiple_of(lax.rem(f + o, n_f) * owned + k * chunk, 128), chunk)

    barrier = pltpu.get_barrier_semaphore()
    for o in range(1, n_f):
        pl.semaphore_signal(barrier, inc=1, device_id=f_peer(o), device_id_type=MESH)
    for o in range(1, n_d):
        pl.semaphore_signal(barrier, inc=1, device_id=d_peer(o), device_id_type=MESH)

    def square(step, total):
        part = x_ref[:, pl.ds(pl.multiple_of(step * 512, 512), 512)].astype(F32)
        part = part * part
        for at in range(0, 512, 128):
            total = total + part[:, at : at + 128]
        return total

    squares = lax.fori_loop(0, model // 512, square, jnp.zeros((tok, 128), F32))
    mean = jnp.sum(squares, axis=1, keepdims=True) / model
    inv[...] = jnp.broadcast_to(lax.rsqrt(mean + EPS_NORM), inv.shape)
    pl.semaphore_wait(barrier, n_f + n_d - 2)

    own_rows = pl.ds(pl.multiple_of(d * rows, 16), rows)
    first, cot_copies, gain_copies = [], [], []
    for o in range(1, n_f):
        at = n_f - o
        first.append(
            send(w_ref.at[own_rows], wall.at[d, at - 1], w_send.at[o - 1], w_recv.at[at - 1], f_peer(o))
        )
    for o in range(1, n_f):
        at = n_f - o
        cot_copies.append(
            send(cot_ref, cot_all.at[at], c_send.at[o - 1], c_recv.at[at - 1], f_peer(o))
        )
        gain_copies.append(
            send(gain_ref, gain_all.at[at], n_send.at[o - 1], n_recv.at[at - 1], f_peer(o))
        )
    cot_all[0] = cot_ref[...]
    gain_all[0] = gain_ref[...]

    col_copies = []
    for k in range(n_k):
        copies = []
        for o in range(n_f):
            normed = (x_ref[:, features(o, k)].astype(F32) * inv[:, :1]).astype(BF16)
            if o == 0:
                cols[k, 0] = normed
                continue
            at = n_f - o
            nb[k, o - 1] = normed
            copies.append(
                send(nb.at[k, o - 1], cols.at[k, at], col_send.at[k, o - 1], col_recv.at[k, at - 1], f_peer(o))
            )
        col_copies.append(copies)

    half = width // 2
    bits = [1 << b for b in reversed(range(n_d.bit_length() - 1))]
    orders = [bits, bits[1::-1] + bits[2:]]
    pending = [first, []]

    def flip(mask):
        index = d
        for bit in bits:
            if mask & bit:
                index = index + bit * (1 - 2 * lax.rem(d // bit, 2))
        return index

    def spread(level):
        for copy in pending[0]:
            copy.wait_recv()
        pending[0] = []
        if level == len(bits):
            return
        for part, order in enumerate(orders):
            held = [0]
            for bit in order[:level]:
                held = held + [mask ^ bit for mask in held]
            bit = order[level]
            for mask in held:
                place = wall.at[flip(mask), :, :, pl.ds(part * half, half)]
                pending[0].append(
                    send(
                        place, place, hyp_send.at[part, (mask ^ bit) - 1], hyp_recv.at[part, (mask ^ bit) - 1],
                        (flip(bit), f),
                    )
                )

    def input_gradient():
        def back_part(o, k):
            if o == 0:
                block = w_ref[k * chunk : (k + 1) * chunk]
            else:
                group = chunk // rows
                block = wall[k * group : (k + 1) * group, o - 1].reshape(chunk, width)
            back = dot_t(cot_ref[...], block)
            return (back * gain_all[o, :, k * chunk : (k + 1) * chunk]).astype(BF16)

        total = jnp.zeros((tok, 128), F32)
        for o in range(n_f):
            for k in range(n_k):
                hat = back_part(o, k)
                place = features(o, k)
                ig_ref[:, place] = hat
                term = hat.astype(F32) * (x_ref[:, place].astype(F32) * inv[:, :1])
                for at in range(0, chunk, 128):
                    total = total + term[:, at : at + 128]
        mean_term = jnp.sum(total, axis=1, keepdims=True) / model

        def finish(step, carry):
            place = pl.ds(pl.multiple_of(step * 512, 512), 512)
            normed = x_ref[:, place].astype(F32) * inv[:, :1]
            hat32 = ig_ref[:, place].astype(F32)
            ig_ref[:, place] = (inv[:, :1] * (hat32 - normed * mean_term)).astype(BF16)
            return carry

        lax.fori_loop(0, model // 512, finish, 0)

    slab_copies = []

    def gather_products(k):
        for copy in slab_copies[k]:
            copy.wait_recv()
        block = slabs[k].reshape(width, chunk)
        if k == 0:
            products[...] = dot_t(block, block)
        else:
            products[...] += dot_t(block, block)

    spread(0)
    for copy in cot_copies + gain_copies:
        copy.wait_recv()
    for k in range(n_k):
        if k == n_k - 1:
            for level in range(min(n_k, len(bits) + 1), len(bits) + 1):
                spread(level)
            input_gradient()
        for copy in col_copies[k]:
            copy.wait_recv()
        place = slice(k * chunk, (k + 1) * chunk)
        cotangent = cot_all[...].reshape(n_f * tok, width)
        columns32 = cols[k].reshape(n_f * tok, chunk).astype(F32)
        scaled = (columns32 * gain_ref[:, place]).astype(BF16)
        grad = lax.dot_general(cotangent, scaled, (((0,), (0,)), ((), ())), preferred_element_type=F32)
        gsend[k] = (grad * scale).astype(BF16).reshape(n_d, slab, chunk)
        copies = []
        for o in range(1, n_d):
            copies.append(
                send(
                    gsend.at[k, lax.rem(d + o, n_d)], slabs.at[k, d],
                    slab_send.at[k, o - 1], slab_recv.at[k, n_d - o - 1], d_peer(o),
                )
            )
        slab_copies.append(copies)
        slabs[k, d] = gsend[k, d]
        back = dot_t(cotangent, w_ref[place])
        gain_grad = jnp.sum(back * columns32, axis=0, keepdims=True) * scale
        g_own[:, place] = gain_grad.astype(BF16).astype(F32)
        if k + 1 < n_k:
            spread(k + 1) if k + 1 <= len(bits) else None
        if k:
            gather_products(k - 1)

    g_copies = []
    for o in range(1, n_d):
        g_copies.append(send(g_own, g_all.at[d], g_send.at[o - 1], g_recv.at[n_d - o - 1], d_peer(o)))
    g_all[d] = g_own[...]
    gather_products(n_k - 1)

    row = lax.broadcasted_iota(jnp.int32, (width, width), 0)
    lane = lax.broadcasted_iota(jnp.int32, (width, width), 1)
    same = lax.rem(row, slab) == lax.rem(lane, slab)
    by_row = jnp.sum(jnp.where(same, products[...], 0.0).reshape(n_d, slab, width), axis=1)
    column = lax.broadcasted_iota(jnp.int32, (n_d, 128), 1)
    gram_w = jnp.zeros((n_d, 128), F32)
    for s in range(n_d):
        part = jnp.sum(by_row[:, s * slab : (s + 1) * slab], axis=1, keepdims=True)
        gram_w = jnp.where(column == s, part, gram_w)
    gram1[d] = gram_w
    one_copies = []
    for o in range(1, n_d):
        one_copies.append(
            send(gram1.at[d], gram1.at[d], one_send.at[o - 1], one_recv.at[n_d - o - 1], d_peer(o))
        )
    for copy in g_copies:
        copy.wait_recv()
    gains = g_all[...].reshape(n_d, owned)
    gram_g = jnp.zeros((n_d, 128), F32)
    for s in range(n_d):
        part = jnp.sum(gains * gains[s : s + 1], axis=1, keepdims=True)
        gram_g = jnp.where(column == s, part, gram_g)
    for copy in one_copies:
        copy.wait_recv()
    total = gram1[0]
    for s in range(1, n_d):
        total = total + gram1[s]
    gram2[f, 0] = total
    gram2[f, 1] = gram_g
    two_copies = []
    for o in range(1, n_f):
        two_copies.append(
            send(gram2.at[f], gram2.at[f], two_send.at[o - 1], two_recv.at[n_f - o - 1], f_peer(o))
        )
    for copy in two_copies:
        copy.wait_recv()
    sum_w, sum_g = gram2[0, 0], gram2[0, 1]
    for s in range(1, n_f):
        sum_w = sum_w + gram2[s, 0]
        sum_g = sum_g + gram2[s, 1]
    coef_w, coef_g = coefficients(sum_w), coefficients(sum_g)
    gain_total = coef_g[0:1, 0:1] * gains[0:1]
    for s in range(1, n_d):
        gain_total = gain_total + coef_g[0:1, s : s + 1] * gains[s : s + 1]
    gu_ref[...] = gain_total.astype(BF16)
    for k in range(n_k):
        weight_total = coef_w[0:1, 0:1] * slabs[k, 0].astype(F32)
        for s in range(1, n_d):
            weight_total = weight_total + coef_w[0:1, s : s + 1] * slabs[k, s].astype(F32)
        wu_ref[:, k * chunk : (k + 1) * chunk] = weight_total.astype(BF16)
    for copy in sent:
        copy.wait_send()


def body(n_d, n_f, layer_input, norm_gain, value_weight, value_cotangent):
    tok, model = layer_input.shape
    owned, width = value_weight.shape
    chunk = min(512, owned)
    n_k = owned // chunk
    rows, slab = owned // n_d, width // n_d
    dma = pltpu.SemaphoreType.DMA
    vmem = pl.BlockSpec(memory_space=pltpu.VMEM)
    pairs = [(n_f - 1,)] * 6 + [(n_k, n_f - 1)] * 2 + [(2, n_d - 1)] * 2 + [(n_k, n_d - 1)] * 2
    pairs += [(n_d - 1,)] * 4 + [(n_f - 1,)] * 2
    input_grad, weight, gain = pl.pallas_call(
        functools.partial(kernel, n_d, n_f, n_k),
        out_shape=(
            jax.ShapeDtypeStruct((tok, model), BF16),
            jax.ShapeDtypeStruct((slab, owned), BF16),
            jax.ShapeDtypeStruct((1, owned), BF16),
        ),
        in_specs=[vmem] * 4,
        out_specs=(vmem,) * 3,
        scratch_shapes=[
            pltpu.VMEM((tok, 128), F32),
            pltpu.VMEM((n_k, n_f - 1, tok, chunk), BF16),
            pltpu.VMEM((n_k, n_f, tok, chunk), BF16),
            pltpu.VMEM((n_f, tok, width), BF16),
            pltpu.VMEM((n_f, 1, owned), F32),
            pltpu.VMEM((n_d, n_f - 1, rows, width), BF16),
            pltpu.VMEM((n_k, n_d, slab, chunk), BF16),
            pltpu.VMEM((n_k, n_d, slab, chunk), BF16),
            pltpu.VMEM((width, width), F32),
            pltpu.VMEM((1, owned), F32),
            pltpu.VMEM((n_d, 1, owned), F32),
            pltpu.VMEM((n_d, n_d, 128), F32),
            pltpu.VMEM((n_f, 2, n_d, 128), F32),
        ]
        + [dma(shape) for shape in pairs],
        compiler_params=pltpu.CompilerParams(
            collective_id=0, has_side_effects=True, vmem_limit_bytes=56 * 1024 * 1024
        ),
        cost_estimate=pl.CostEstimate(
            flops=8 * tok * model * width, bytes_accessed=8 * tok * model, transcendentals=0
        ),
    )(layer_input, norm_gain.reshape(1, owned), value_weight, value_cotangent)
    return (input_grad, weight.T, gain.reshape(owned))


def solution(mesh):
    in_specs = (P(("dp", "fsdp"), None), P("fsdp"), P("fsdp", None), P(("dp", "fsdp"), None))
    out_specs = (P(("dp", "fsdp"), None), P("fsdp", "dp"), P("fsdp"))
    inner = functools.partial(body, mesh.shape["dp"], mesh.shape["fsdp"])
    return jax.shard_map(inner, mesh=mesh, in_specs=in_specs, out_specs=out_specs, check_vma=False)
```

```python
import functools
import math

import jax
import jax.numpy as jnp
from jax import lax
from jax.experimental import pallas as pl
from jax.experimental.pallas import tpu as pltpu
from jax.sharding import PartitionSpec as P

EPS_NORM = 1e-05
EPS_SUM = 1e-06
MESH = pl.DeviceIdType.MESH
F32 = jnp.float32
BF16 = jnp.bfloat16


def dot_t(a, b):
    return lax.dot_general(a, b, (((1,), (1,)), ((), ())), preferred_element_type=F32)


def coefficients(gram):
    count, lanes = gram.shape
    row = lax.broadcasted_iota(jnp.int32, gram.shape, 0)
    lane = lax.broadcasted_iota(jnp.int32, gram.shape, 1)
    coef = jnp.where(row == lane, 1.0, 0.0).astype(F32)
    stride = count // 2
    while stride:
        row_set = lax.rem(row // stride, 2) == 1
        lane_set = lax.rem(lane // stride, 2) == 1
        row_partner = jnp.where(row_set, row - stride, row + stride)

        def swap_rows(block):
            down = pltpu.roll(block, stride, 0)
            up = pltpu.roll(block, count - stride, 0)
            return jnp.where(row_set, down, up)

        def swap_lanes(block):
            down = pltpu.roll(block, stride, 1)
            up = pltpu.roll(block, lanes - stride, 1)
            return jnp.where(lane_set, down, up)

        own = jnp.where(row == lane, gram, 0.0)
        meet = jnp.where(row_partner == lane, gram, 0.0)

        def weights(axis):
            norm = jnp.maximum(jnp.sum(own, axis=axis, keepdims=True), 0.0)
            inner = jnp.sum(meet, axis=axis, keepdims=True)
            return jnp.broadcast_to(1.0 - inner / (2.0 * (norm + EPS_SUM)), gram.shape)

        mine, mine_lane = weights(1), weights(0)
        other, other_lane = swap_rows(mine), swap_lanes(mine_lane)
        coef = mine * coef + other * swap_rows(coef)
        gram = mine * gram + other * swap_rows(gram)
        gram = mine_lane * gram + other_lane * swap_lanes(gram)
        stride //= 2
    return coef


def kernel(
    n_d, n_f, n_k,
    x_ref, gain_ref, w_ref, cot_ref,
    ig_ref, wu_ref, gu_ref,
    inv, nb, cols, cot_all, gain_all, wall, gsend, slabs, cot_turned, products, g_own, g_all, gram1, gram2,
    w_send, w_recv, c_send, c_recv, n_send, n_recv, col_send, col_recv, hyp_send, hyp_recv,
    slab_send, slab_recv, g_send, g_recv, one_send, one_recv, two_send, two_recv,
):
    d, f = lax.axis_index("dp"), lax.axis_index("fsdp")
    tok, model = x_ref.shape
    owned, width = w_ref.shape
    chunk = owned // n_k
    rows = owned // n_d
    slab = width // n_d
    scale = 1.0 / math.sqrt(n_f * tok)
    sent = []

    def f_peer(o):
        return (d, lax.rem(f + o, n_f))

    def d_peer(o):
        return (lax.rem(d + o, n_d), f)

    def send(src, dst, send_sem, recv_sem, device):
        copy = pltpu.make_async_remote_copy(
            src_ref=src, dst_ref=dst, send_sem=send_sem, recv_sem=recv_sem,
            device_id=device, device_id_type=MESH,
        )
        copy.start()
        sent.append(copy)
        return copy

    def left(copies):
        for copy in copies:
            copy.wait_send()
        sent[:] = [copy for copy in sent if all(copy is not gone for gone in copies)]

    def features(o, k):
        return pl.ds(pl.multiple_of(lax.rem(f + o, n_f) * owned + k * chunk, 128), chunk)

    barrier = pltpu.get_barrier_semaphore()
    for o in range(1, n_f):
        pl.semaphore_signal(barrier, inc=1, device_id=f_peer(o), device_id_type=MESH)
    for o in range(1, n_d):
        pl.semaphore_signal(barrier, inc=1, device_id=d_peer(o), device_id_type=MESH)

    def square(step, total):
        part = x_ref[:, pl.ds(pl.multiple_of(step * 512, 512), 512)].astype(F32)
        part = part * part
        for at in range(0, 512, 128):
            total = total + part[:, at : at + 128]
        return total

    squares = lax.fori_loop(0, model // 512, square, jnp.zeros((tok, 128), F32))
    mean = jnp.sum(squares, axis=1, keepdims=True) / model
    inv[...] = jnp.broadcast_to(lax.rsqrt(mean + EPS_NORM), inv.shape)
    pl.semaphore_wait(barrier, n_f + n_d - 2)

    own_rows = pl.ds(pl.multiple_of(d * rows, 16), rows)
    first, cot_copies, gain_copies = [], [], []
    for o in range(1, n_f):
        at = n_f - o
        first.append(
            send(w_ref.at[own_rows], wall.at[d, at - 1], w_send.at[o - 1], w_recv.at[at - 1], f_peer(o))
        )
    for o in range(1, n_f):
        at = n_f - o
        cot_copies.append(
            send(cot_ref, cot_all.at[at], c_send.at[o - 1], c_recv.at[at - 1], f_peer(o))
        )
        gain_copies.append(
            send(gain_ref, gain_all.at[at], n_send.at[o - 1], n_recv.at[at - 1], f_peer(o))
        )
    cot_all[0] = cot_ref[...]
    gain_all[0] = gain_ref[...]

    col_copies = []
    for k in range(n_k):
        for o in range(n_f):
            normed = (x_ref[:, features(o, k)].astype(F32) * inv[:, :1]).astype(BF16)
            if o == 0:
                cols[k, 0] = normed
            else:
                nb[k, o - 1] = normed

    def send_columns(k):
        copies = []
        for o in range(1, n_f):
            at = n_f - o
            copies.append(
                send(nb.at[k, o - 1], cols.at[k, at], col_send.at[k, o - 1], col_recv.at[k, at - 1], f_peer(o))
            )
        col_copies.append(copies)

    half = width // 2
    bits = [1 << b for b in reversed(range(n_d.bit_length() - 1))]
    orders = [bits, bits[1::-1] + bits[2:]]
    pending = [first, []]

    def flip(mask):
        index = d
        for bit in bits:
            if mask & bit:
                index = index + bit * (1 - 2 * lax.rem(d // bit, 2))
        return index

    def spread(level):
        for copy in pending[0]:
            copy.wait_recv()
        pending[0] = []
        if level == len(bits):
            return
        for part, order in enumerate(orders):
            held = [0]
            for bit in order[:level]:
                held = held + [mask ^ bit for mask in held]
            bit = order[level]
            for mask in held:
                place = wall.at[flip(mask), :, :, pl.ds(part * half, half)]
                pending[0].append(
                    send(
                        place, place, hyp_send.at[part, (mask ^ bit) - 1], hyp_recv.at[part, (mask ^ bit) - 1],
                        (flip(bit), f),
                    )
                )

    def input_gradient():
        def back_part(o, k):
            if o == 0:
                block = w_ref[k * chunk : (k + 1) * chunk]
            else:
                group = chunk // rows
                block = wall[k * group : (k + 1) * group, o - 1].reshape(chunk, width)
            back = dot_t(cot_ref[...], block)
            return (back * gain_all[o, :, k * chunk : (k + 1) * chunk]).astype(BF16)

        total = jnp.zeros((tok, 128), F32)
        for o in range(n_f):
            for k in range(n_k):
                hat = back_part(o, k)
                place = features(o, k)
                ig_ref[:, place] = hat
                term = hat.astype(F32) * (x_ref[:, place].astype(F32) * inv[:, :1])
                for at in range(0, chunk, 128):
                    total = total + term[:, at : at + 128]
        mean_term = jnp.sum(total, axis=1, keepdims=True) / model

        def finish(step, carry):
            place = pl.ds(pl.multiple_of(step * 512, 512), 512)
            normed = x_ref[:, place].astype(F32) * inv[:, :1]
            hat32 = ig_ref[:, place].astype(F32)
            ig_ref[:, place] = (inv[:, :1] * (hat32 - normed * mean_term)).astype(BF16)
            return carry

        lax.fori_loop(0, model // 512, finish, 0)

    slab_copies = []

    def gather_products(k):
        for copy in slab_copies[k]:
            copy.wait_recv()
        block = slabs[k].reshape(width, chunk)
        if k == 0:
            products[...] = dot_t(block, block)
        else:
            products[...] += dot_t(block, block)

    levels = len(bits)
    spread(0)
    send_columns(0)
    spread(1)
    done = 1
    for copy in cot_copies + gain_copies:
        copy.wait_recv()
    cot_turned[...] = cot_all[...].reshape(n_f * tok, width).T
    for k in range(n_k):
        if k + 1 < n_k:
            left(col_copies[k])
            send_columns(k + 1)
        if k == n_k - 1:
            while done < levels:
                done += 1
                spread(done)
            input_gradient()
        for copy in col_copies[k]:
            copy.wait_recv()
        place = slice(k * chunk, (k + 1) * chunk)
        cotangent = cot_all[...].reshape(n_f * tok, width)
        columns32 = cols[k].reshape(n_f * tok, chunk).astype(F32)
        scaled = (columns32 * gain_ref[:, place]).astype(BF16)
        grad = jnp.dot(cot_turned[...], scaled, preferred_element_type=F32)
        gsend[k] = (grad * scale).astype(BF16).reshape(n_d, slab, chunk)
        copies = []
        for o in range(1, n_d):
            copies.append(
                send(
                    gsend.at[k, lax.rem(d + o, n_d)], slabs.at[k, d],
                    slab_send.at[k, o - 1], slab_recv.at[k, n_d - o - 1], d_peer(o),
                )
            )
        slab_copies.append(copies)
        slabs[k, d] = gsend[k, d]
        back = dot_t(cotangent, w_ref[place])
        gain_grad = jnp.sum(back * columns32, axis=0, keepdims=True) * scale
        g_own[:, place] = gain_grad.astype(BF16).astype(F32)
        if 0 < k < n_k - 1 and done < levels:
            done += 1
            spread(done)
        if k:
            gather_products(k - 1)

    g_copies = []
    for o in range(1, n_d):
        g_copies.append(send(g_own, g_all.at[d], g_send.at[o - 1], g_recv.at[n_d - o - 1], d_peer(o)))
    g_all[d] = g_own[...]
    gather_products(n_k - 1)

    row = lax.broadcasted_iota(jnp.int32, (width, width), 0)
    lane = lax.broadcasted_iota(jnp.int32, (width, width), 1)
    same = lax.rem(row, slab) == lax.rem(lane, slab)
    by_row = jnp.sum(jnp.where(same, products[...], 0.0).reshape(n_d, slab, width), axis=1)
    column = lax.broadcasted_iota(jnp.int32, (n_d, 128), 1)
    gram_w = jnp.zeros((n_d, 128), F32)
    for s in range(n_d):
        part = jnp.sum(by_row[:, s * slab : (s + 1) * slab], axis=1, keepdims=True)
        gram_w = jnp.where(column == s, part, gram_w)
    gram1[d] = gram_w
    one_copies = []
    for o in range(1, n_d):
        one_copies.append(
            send(gram1.at[d], gram1.at[d], one_send.at[o - 1], one_recv.at[n_d - o - 1], d_peer(o))
        )
    for copy in g_copies:
        copy.wait_recv()
    gains = g_all[...].reshape(n_d, owned)
    gram_g = jnp.zeros((n_d, 128), F32)
    for s in range(n_d):
        part = jnp.sum(gains * gains[s : s + 1], axis=1, keepdims=True)
        gram_g = jnp.where(column == s, part, gram_g)
    for copy in one_copies:
        copy.wait_recv()
    total = gram1[0]
    for s in range(1, n_d):
        total = total + gram1[s]
    gram2[f, 0] = total
    gram2[f, 1] = gram_g
    two_copies = []
    for o in range(1, n_f):
        two_copies.append(
            send(gram2.at[f], gram2.at[f], two_send.at[o - 1], two_recv.at[n_f - o - 1], f_peer(o))
        )
    for copy in two_copies:
        copy.wait_recv()
    sum_w, sum_g = gram2[0, 0], gram2[0, 1]
    for s in range(1, n_f):
        sum_w = sum_w + gram2[s, 0]
        sum_g = sum_g + gram2[s, 1]
    coef_w, coef_g = coefficients(sum_w), coefficients(sum_g)
    gain_total = coef_g[0:1, 0:1] * gains[0:1]
    for s in range(1, n_d):
        gain_total = gain_total + coef_g[0:1, s : s + 1] * gains[s : s + 1]
    gu_ref[...] = gain_total.astype(BF16)
    for k in range(n_k):
        weight_total = coef_w[0:1, 0:1] * slabs[k, 0].astype(F32)
        for s in range(1, n_d):
            weight_total = weight_total + coef_w[0:1, s : s + 1] * slabs[k, s].astype(F32)
        wu_ref[:, k * chunk : (k + 1) * chunk] = weight_total.astype(BF16)
    for copy in sent:
        copy.wait_send()


def body(n_d, n_f, layer_input, norm_gain, value_weight, value_cotangent):
    tok, model = layer_input.shape
    owned, width = value_weight.shape
    chunk = min(512, owned)
    n_k = owned // chunk
    rows, slab = owned // n_d, width // n_d
    dma = pltpu.SemaphoreType.DMA
    vmem = pl.BlockSpec(memory_space=pltpu.VMEM)
    pairs = [(n_f - 1,)] * 6 + [(n_k, n_f - 1)] * 2 + [(2, n_d - 1)] * 2 + [(n_k, n_d - 1)] * 2
    pairs += [(n_d - 1,)] * 4 + [(n_f - 1,)] * 2
    input_grad, weight, gain = pl.pallas_call(
        functools.partial(kernel, n_d, n_f, n_k),
        out_shape=(
            jax.ShapeDtypeStruct((tok, model), BF16),
            jax.ShapeDtypeStruct((slab, owned), BF16),
            jax.ShapeDtypeStruct((1, owned), BF16),
        ),
        in_specs=[vmem] * 4,
        out_specs=(vmem,) * 3,
        scratch_shapes=[
            pltpu.VMEM((tok, 128), F32),
            pltpu.VMEM((n_k, n_f - 1, tok, chunk), BF16),
            pltpu.VMEM((n_k, n_f, tok, chunk), BF16),
            pltpu.VMEM((n_f, tok, width), BF16),
            pltpu.VMEM((n_f, 1, owned), F32),
            pltpu.VMEM((n_d, n_f - 1, rows, width), BF16),
            pltpu.VMEM((n_k, n_d, slab, chunk), BF16),
            pltpu.VMEM((n_k, n_d, slab, chunk), BF16),
            pltpu.VMEM((width, n_f * tok), BF16),
            pltpu.VMEM((width, width), F32),
            pltpu.VMEM((1, owned), F32),
            pltpu.VMEM((n_d, 1, owned), F32),
            pltpu.VMEM((n_d, n_d, 128), F32),
            pltpu.VMEM((n_f, 2, n_d, 128), F32),
        ]
        + [dma(shape) for shape in pairs],
        compiler_params=pltpu.CompilerParams(
            collective_id=0, has_side_effects=True, vmem_limit_bytes=56 * 1024 * 1024
        ),
        cost_estimate=pl.CostEstimate(
            flops=8 * tok * model * width, bytes_accessed=8 * tok * model, transcendentals=0
        ),
    )(layer_input, norm_gain.reshape(1, owned), value_weight, value_cotangent)
    return (input_grad, weight.T, gain.reshape(owned))


def solution(mesh):
    in_specs = (P(("dp", "fsdp"), None), P("fsdp"), P("fsdp", None), P(("dp", "fsdp"), None))
    out_specs = (P(("dp", "fsdp"), None), P("fsdp", "dp"), P("fsdp"))
    inner = functools.partial(body, mesh.shape["dp"], mesh.shape["fsdp"])
    return jax.shard_map(inner, mesh=mesh, in_specs=in_specs, out_specs=out_specs, check_vma=False)
```

```python
import functools
import math

import jax
import jax.numpy as jnp
from jax import lax
from jax.experimental import pallas as pl
from jax.experimental.pallas import tpu as pltpu
from jax.sharding import PartitionSpec as P

EPS_NORM = 1e-05
EPS_SUM = 1e-06
MESH = pl.DeviceIdType.MESH
F32 = jnp.float32
BF16 = jnp.bfloat16


def dot_t(a, b):
    return lax.dot_general(a, b, (((1,), (1,)), ((), ())), preferred_element_type=F32)


def coefficients(gram):
    count, lanes = gram.shape
    row = lax.broadcasted_iota(jnp.int32, gram.shape, 0)
    lane = lax.broadcasted_iota(jnp.int32, gram.shape, 1)
    coef = jnp.where(row == lane, 1.0, 0.0).astype(F32)
    stride = count // 2
    while stride:
        row_set = lax.rem(row // stride, 2) == 1
        lane_set = lax.rem(lane // stride, 2) == 1
        row_partner = jnp.where(row_set, row - stride, row + stride)

        def swap_rows(block):
            down = pltpu.roll(block, stride, 0)
            up = pltpu.roll(block, count - stride, 0)
            return jnp.where(row_set, down, up)

        def swap_lanes(block):
            down = pltpu.roll(block, stride, 1)
            up = pltpu.roll(block, lanes - stride, 1)
            return jnp.where(lane_set, down, up)

        own = jnp.where(row == lane, gram, 0.0)
        meet = jnp.where(row_partner == lane, gram, 0.0)

        def weights(axis):
            norm = jnp.maximum(jnp.sum(own, axis=axis, keepdims=True), 0.0)
            inner = jnp.sum(meet, axis=axis, keepdims=True)
            return jnp.broadcast_to(1.0 - inner / (2.0 * (norm + EPS_SUM)), gram.shape)

        mine, mine_lane = weights(1), weights(0)
        other, other_lane = swap_rows(mine), swap_lanes(mine_lane)
        coef = mine * coef + other * swap_rows(coef)
        gram = mine * gram + other * swap_rows(gram)
        gram = mine_lane * gram + other_lane * swap_lanes(gram)
        stride //= 2
    return coef


def kernel(
    n_d, n_f, n_k,
    x_ref, gain_ref, w_ref, cot_ref,
    hat_ref, inv, mean_ref, wu_ref, gu_ref,
    nb, cols, cot_all, gain_all, wall, gsend, slabs, cot_turned, products, g_own, g_all, gram1, gram2,
    w_send, w_recv, c_send, c_recv, n_send, n_recv, col_send, col_recv, hyp_send, hyp_recv,
    slab_send, slab_recv, g_send, g_recv, one_send, one_recv, two_send, two_recv,
):
    d, f = lax.axis_index("dp"), lax.axis_index("fsdp")
    tok, model = x_ref.shape
    owned, width = w_ref.shape
    chunk = owned // n_k
    rows = owned // n_d
    slab = width // n_d
    scale = 1.0 / math.sqrt(n_f * tok)
    sent = []

    def f_peer(o):
        return (d, lax.rem(f + o, n_f))

    def d_peer(o):
        return (lax.rem(d + o, n_d), f)

    def send(src, dst, send_sem, recv_sem, device):
        copy = pltpu.make_async_remote_copy(
            src_ref=src, dst_ref=dst, send_sem=send_sem, recv_sem=recv_sem,
            device_id=device, device_id_type=MESH,
        )
        copy.start()
        sent.append(copy)
        return copy

    def left(copies):
        for copy in copies:
            copy.wait_send()
        sent[:] = [copy for copy in sent if all(copy is not gone for gone in copies)]

    def features(o, k):
        return pl.ds(pl.multiple_of(lax.rem(f + o, n_f) * owned + k * chunk, 128), chunk)

    barrier = pltpu.get_barrier_semaphore()
    for o in range(1, n_f):
        pl.semaphore_signal(barrier, inc=1, device_id=f_peer(o), device_id_type=MESH)
    for o in range(1, n_d):
        pl.semaphore_signal(barrier, inc=1, device_id=d_peer(o), device_id_type=MESH)

    pl.semaphore_wait(barrier, n_f + n_d - 2)

    own_rows = pl.ds(pl.multiple_of(d * rows, 16), rows)
    first, cot_copies, gain_copies = [], [], []
    for o in range(1, n_f):
        at = n_f - o
        first.append(
            send(w_ref.at[own_rows], wall.at[d, at - 1], w_send.at[o - 1], w_recv.at[at - 1], f_peer(o))
        )
    for o in range(1, n_f):
        at = n_f - o
        cot_copies.append(
            send(cot_ref, cot_all.at[at], c_send.at[o - 1], c_recv.at[at - 1], f_peer(o))
        )
        gain_copies.append(
            send(gain_ref, gain_all.at[at], n_send.at[o - 1], n_recv.at[at - 1], f_peer(o))
        )
    cot_all[0] = cot_ref[...]
    gain_all[0] = gain_ref[...]

    def square(step, total):
        part = x_ref[:, pl.ds(pl.multiple_of(step * 512, 512), 512)].astype(F32)
        part = part * part
        for at in range(0, 512, 128):
            total = total + part[:, at : at + 128]
        return total

    squares = lax.fori_loop(0, model // 512, square, jnp.zeros((tok, 128), F32))
    mean = jnp.sum(squares, axis=1, keepdims=True) / model
    inv[...] = jnp.broadcast_to(lax.rsqrt(mean + EPS_NORM), inv.shape)

    col_copies = []

    def send_columns(k):
        copies = []
        for o in range(n_f):
            normed = (x_ref[:, features(o, k)].astype(F32) * inv[:, :1]).astype(BF16)
            if o == 0:
                cols[k, 0] = normed
                continue
            at = n_f - o
            nb[k, o - 1] = normed
            copies.append(
                send(nb.at[k, o - 1], cols.at[k, at], col_send.at[k, o - 1], col_recv.at[k, at - 1], f_peer(o))
            )
        col_copies.append(copies)

    half = width // 2
    bits = [1 << b for b in reversed(range(n_d.bit_length() - 1))]
    orders = [bits, bits[1::-1] + bits[2:]]
    pending = [first, []]

    def flip(mask):
        index = d
        for bit in bits:
            if mask & bit:
                index = index + bit * (1 - 2 * lax.rem(d // bit, 2))
        return index

    def spread(level):
        for copy in pending[0]:
            copy.wait_recv()
        pending[0] = []
        if level == len(bits):
            return
        for part, order in enumerate(orders):
            held = [0]
            for bit in order[:level]:
                held = held + [mask ^ bit for mask in held]
            bit = order[level]
            for mask in held:
                place = wall.at[flip(mask), :, :, pl.ds(part * half, half)]
                pending[0].append(
                    send(
                        place, place, hyp_send.at[part, (mask ^ bit) - 1], hyp_recv.at[part, (mask ^ bit) - 1],
                        (flip(bit), f),
                    )
                )

    def hat_gradient():
        def back_part(o, k):
            if o == 0:
                block = w_ref[k * chunk : (k + 1) * chunk]
            else:
                group = chunk // rows
                block = wall[k * group : (k + 1) * group, o - 1].reshape(chunk, width)
            back = dot_t(cot_ref[...], block)
            return (back * gain_all[o, :, k * chunk : (k + 1) * chunk]).astype(BF16)

        total = jnp.zeros((tok, 128), F32)
        for o in range(n_f):
            for k in range(n_k):
                hat = back_part(o, k)
                place = features(o, k)
                hat_ref[:, place] = hat
                term = hat.astype(F32) * (x_ref[:, place].astype(F32) * inv[:, :1])
                for at in range(0, chunk, 128):
                    total = total + term[:, at : at + 128]
        mean_term = jnp.sum(total, axis=1, keepdims=True) / model
        mean_ref[...] = jnp.broadcast_to(mean_term, mean_ref.shape)

    slab_copies = []

    def gather_products(k):
        for copy in slab_copies[k]:
            copy.wait_recv()
        block = slabs[k].reshape(width, chunk)
        if k == 0:
            products[...] = dot_t(block, block)
        else:
            products[...] += dot_t(block, block)

    levels = len(bits)
    send_columns(0)
    if n_k > 1:
        send_columns(1)
    spread(0)
    done = 0
    for copy in cot_copies + gain_copies:
        copy.wait_recv()
    cot_turned[...] = cot_all[...].reshape(n_f * tok, width).T
    for k in range(n_k):
        for copy in col_copies[k]:
            copy.wait_recv()
        if k + 2 < n_k:
            left(col_copies[k])
            send_columns(k + 2)
        place = slice(k * chunk, (k + 1) * chunk)
        cotangent = cot_all[...].reshape(n_f * tok, width)
        columns32 = cols[k].reshape(n_f * tok, chunk).astype(F32)
        scaled = (columns32 * gain_ref[:, place]).astype(BF16)
        grad = jnp.dot(cot_turned[...], scaled, preferred_element_type=F32)
        gsend[k] = (grad * scale).astype(BF16).reshape(n_d, slab, chunk)
        copies = []
        for o in range(1, n_d):
            copies.append(
                send(
                    gsend.at[k, lax.rem(d + o, n_d)], slabs.at[k, d],
                    slab_send.at[k, o - 1], slab_recv.at[k, n_d - o - 1], d_peer(o),
                )
            )
        slab_copies.append(copies)
        slabs[k, d] = gsend[k, d]
        back = dot_t(cotangent, w_ref[place])
        gain_grad = jnp.sum(back * columns32, axis=0, keepdims=True) * scale
        g_own[:, place] = gain_grad.astype(BF16).astype(F32)
        if done < levels:
            done += 1
            spread(done)
        if k:
            gather_products(k - 1)

    g_copies = []
    for o in range(1, n_d):
        g_copies.append(send(g_own, g_all.at[d], g_send.at[o - 1], g_recv.at[n_d - o - 1], d_peer(o)))
    g_all[d] = g_own[...]
    while done < levels:
        done += 1
        spread(done)
    hat_gradient()
    gather_products(n_k - 1)

    row = lax.broadcasted_iota(jnp.int32, (width, width), 0)
    lane = lax.broadcasted_iota(jnp.int32, (width, width), 1)
    same = lax.rem(row, slab) == lax.rem(lane, slab)
    by_row = jnp.sum(jnp.where(same, products[...], 0.0).reshape(n_d, slab, width), axis=1)
    column = lax.broadcasted_iota(jnp.int32, (n_d, 128), 1)
    gram_w = jnp.zeros((n_d, 128), F32)
    for s in range(n_d):
        part = jnp.sum(by_row[:, s * slab : (s + 1) * slab], axis=1, keepdims=True)
        gram_w = jnp.where(column == s, part, gram_w)
    gram1[d] = gram_w
    one_copies = []
    for o in range(1, n_d):
        one_copies.append(
            send(gram1.at[d], gram1.at[d], one_send.at[o - 1], one_recv.at[n_d - o - 1], d_peer(o))
        )
    for copy in g_copies:
        copy.wait_recv()
    gains = g_all[...].reshape(n_d, owned)
    gram_g = jnp.zeros((n_d, 128), F32)
    for s in range(n_d):
        part = jnp.sum(gains * gains[s : s + 1], axis=1, keepdims=True)
        gram_g = jnp.where(column == s, part, gram_g)
    for copy in one_copies:
        copy.wait_recv()
    total = gram1[0]
    for s in range(1, n_d):
        total = total + gram1[s]
    gram2[f, 0] = total
    gram2[f, 1] = gram_g
    two_copies = []
    for o in range(1, n_f):
        two_copies.append(
            send(gram2.at[f], gram2.at[f], two_send.at[o - 1], two_recv.at[n_f - o - 1], f_peer(o))
        )
    for copy in two_copies:
        copy.wait_recv()
    sum_w, sum_g = gram2[0, 0], gram2[0, 1]
    for s in range(1, n_f):
        sum_w = sum_w + gram2[s, 0]
        sum_g = sum_g + gram2[s, 1]
    coef_w, coef_g = coefficients(sum_w), coefficients(sum_g)
    gain_total = coef_g[0:1, 0:1] * gains[0:1]
    for s in range(1, n_d):
        gain_total = gain_total + coef_g[0:1, s : s + 1] * gains[s : s + 1]
    for at in range(owned // 128):
        gu_ref[at : at + 1] = gain_total[:, at * 128 : (at + 1) * 128]
    for k in range(n_k):
        weight_total = coef_w[0:1, 0:1] * slabs[k, 0].astype(F32)
        for s in range(1, n_d):
            weight_total = weight_total + coef_w[0:1, s : s + 1] * slabs[k, s].astype(F32)
        wu_ref[:, k * chunk : (k + 1) * chunk] = weight_total.astype(BF16)
    for copy in sent:
        copy.wait_send()


def body(n_d, n_f, layer_input, norm_gain, value_weight, value_cotangent):
    tok, model = layer_input.shape
    owned, width = value_weight.shape
    chunk = min(512, owned)
    n_k = owned // chunk
    rows, slab = owned // n_d, width // n_d
    dma = pltpu.SemaphoreType.DMA
    vmem = pl.BlockSpec(memory_space=pltpu.VMEM)
    pairs = [(n_f - 1,)] * 6 + [(n_k, n_f - 1)] * 2 + [(2, n_d - 1)] * 2 + [(n_k, n_d - 1)] * 2
    pairs += [(n_d - 1,)] * 4 + [(n_f - 1,)] * 2
    hat, inverse_rms, mean_term, weight, gain = pl.pallas_call(
        functools.partial(kernel, n_d, n_f, n_k),
        out_shape=(
            jax.ShapeDtypeStruct((tok, model), BF16),
            jax.ShapeDtypeStruct((tok, 128), F32),
            jax.ShapeDtypeStruct((tok, 128), F32),
            jax.ShapeDtypeStruct((slab, owned), BF16),
            jax.ShapeDtypeStruct((owned // 128, 128), F32),
        ),
        in_specs=[vmem] * 4,
        out_specs=(vmem,) * 5,
        scratch_shapes=[
            pltpu.VMEM((n_k, n_f - 1, tok, chunk), BF16),
            pltpu.VMEM((n_k, n_f, tok, chunk), BF16),
            pltpu.VMEM((n_f, tok, width), BF16),
            pltpu.VMEM((n_f, 1, owned), F32),
            pltpu.VMEM((n_d, n_f - 1, rows, width), BF16),
            pltpu.VMEM((n_k, n_d, slab, chunk), BF16),
            pltpu.VMEM((n_k, n_d, slab, chunk), BF16),
            pltpu.VMEM((width, n_f * tok), BF16),
            pltpu.VMEM((width, width), F32),
            pltpu.VMEM((1, owned), F32),
            pltpu.VMEM((n_d, 1, owned), F32),
            pltpu.VMEM((n_d, n_d, 128), F32),
            pltpu.VMEM((n_f, 2, n_d, 128), F32),
        ]
        + [dma(shape) for shape in pairs],
        compiler_params=pltpu.CompilerParams(
            collective_id=0, has_side_effects=True, vmem_limit_bytes=56 * 1024 * 1024
        ),
        cost_estimate=pl.CostEstimate(
            flops=8 * tok * model * width, bytes_accessed=8 * tok * model, transcendentals=0
        ),
    )(layer_input, norm_gain.reshape(1, owned), value_weight, value_cotangent)
    inverse_rms = inverse_rms[:, :1]
    normed = layer_input.astype(F32) * inverse_rms
    input_grad = (inverse_rms * (hat.astype(F32) - normed * mean_term[:, :1])).astype(BF16)
    return (input_grad, weight.T, gain.reshape(owned).astype(BF16))


def solution(mesh):
    in_specs = (P(("dp", "fsdp"), None), P("fsdp"), P("fsdp", None), P(("dp", "fsdp"), None))
    out_specs = (P(("dp", "fsdp"), None), P("fsdp", "dp"), P("fsdp"))
    inner = functools.partial(body, mesh.shape["dp"], mesh.shape["fsdp"])
    return jax.shard_map(inner, mesh=mesh, in_specs=in_specs, out_specs=out_specs, check_vma=False)
```

```python
import functools
import math

import jax
import jax.numpy as jnp
from jax import lax
from jax.experimental import pallas as pl
from jax.experimental.pallas import tpu as pltpu
from jax.sharding import PartitionSpec as P

EPS_NORM = 1e-05
EPS_SUM = 1e-06
MESH = pl.DeviceIdType.MESH
F32 = jnp.float32
BF16 = jnp.bfloat16


def dot_t(a, b):
    return lax.dot_general(a, b, (((1,), (1,)), ((), ())), preferred_element_type=F32)


def coefficients(gram):
    count, lanes = gram.shape
    row = lax.broadcasted_iota(jnp.int32, gram.shape, 0)
    lane = lax.broadcasted_iota(jnp.int32, gram.shape, 1)
    coef = jnp.where(row == lane, 1.0, 0.0).astype(F32)
    stride = count // 2
    while stride:
        row_set = lax.rem(row // stride, 2) == 1
        lane_set = lax.rem(lane // stride, 2) == 1
        row_partner = jnp.where(row_set, row - stride, row + stride)

        def swap_rows(block):
            down = pltpu.roll(block, stride, 0)
            up = pltpu.roll(block, count - stride, 0)
            return jnp.where(row_set, down, up)

        def swap_lanes(block):
            down = pltpu.roll(block, stride, 1)
            up = pltpu.roll(block, lanes - stride, 1)
            return jnp.where(lane_set, down, up)

        own = jnp.where(row == lane, gram, 0.0)
        meet = jnp.where(row_partner == lane, gram, 0.0)

        def weights(axis):
            norm = jnp.maximum(jnp.sum(own, axis=axis, keepdims=True), 0.0)
            inner = jnp.sum(meet, axis=axis, keepdims=True)
            return jnp.broadcast_to(1.0 - inner / (2.0 * (norm + EPS_SUM)), gram.shape)

        mine, mine_lane = weights(1), weights(0)
        other, other_lane = swap_rows(mine), swap_lanes(mine_lane)
        coef = mine * coef + other * swap_rows(coef)
        gram = mine * gram + other * swap_rows(gram)
        gram = mine_lane * gram + other_lane * swap_lanes(gram)
        stride //= 2
    return coef


def kernel(
    n_d, n_f, n_k,
    x_ref, gain_ref, w_ref, cot_ref,
    ig_ref, wu_ref, gu_ref,
    inv, means, nb, cols, cot_all, gain_all, wall, gsend, slabs, cot_turned, products, g_own, g_all, gram1, gram2,
    w_send, w_recv, c_send, c_recv, n_send, n_recv, col_send, col_recv, hyp_send, hyp_recv,
    slab_send, slab_recv, g_send, g_recv, one_send, one_recv, two_send, two_recv,
):
    d, f = lax.axis_index("dp"), lax.axis_index("fsdp")
    tok, model = x_ref.shape
    owned, width = w_ref.shape
    chunk = owned // n_k
    rows = owned // n_d
    slab = width // n_d
    scale = 1.0 / math.sqrt(n_f * tok)
    sent = []

    def f_peer(o):
        return (d, lax.rem(f + o, n_f))

    def d_peer(o):
        return (lax.rem(d + o, n_d), f)

    def send(src, dst, send_sem, recv_sem, device):
        copy = pltpu.make_async_remote_copy(
            src_ref=src, dst_ref=dst, send_sem=send_sem, recv_sem=recv_sem,
            device_id=device, device_id_type=MESH,
        )
        copy.start()
        sent.append(copy)
        return copy

    def left(copies):
        for copy in copies:
            copy.wait_send()
        sent[:] = [copy for copy in sent if all(copy is not gone for gone in copies)]

    def features(o, k):
        return pl.ds(pl.multiple_of(lax.rem(f + o, n_f) * owned + k * chunk, 128), chunk)

    barrier = pltpu.get_barrier_semaphore()
    for o in range(1, n_f):
        pl.semaphore_signal(barrier, inc=1, device_id=f_peer(o), device_id_type=MESH)
    for o in range(1, n_d):
        pl.semaphore_signal(barrier, inc=1, device_id=d_peer(o), device_id_type=MESH)

    pl.semaphore_wait(barrier, n_f + n_d - 2)

    own_rows = pl.ds(pl.multiple_of(d * rows, 16), rows)
    first, cot_copies, gain_copies = [], [], []
    for o in range(1, n_f):
        at = n_f - o
        first.append(
            send(w_ref.at[own_rows], wall.at[d, at - 1], w_send.at[o - 1], w_recv.at[at - 1], f_peer(o))
        )
    for o in range(1, n_f):
        at = n_f - o
        cot_copies.append(
            send(cot_ref, cot_all.at[at], c_send.at[o - 1], c_recv.at[at - 1], f_peer(o))
        )
        gain_copies.append(
            send(gain_ref, gain_all.at[at], n_send.at[o - 1], n_recv.at[at - 1], f_peer(o))
        )
    cot_all[0] = cot_ref[...]
    gain_all[0] = gain_ref[...]

    def square(step, total):
        part = x_ref[:, pl.ds(pl.multiple_of(step * 512, 512), 512)].astype(F32)
        part = part * part
        for at in range(0, 512, 128):
            total = total + part[:, at : at + 128]
        return total

    squares = lax.fori_loop(0, model // 512, square, jnp.zeros((tok, 128), F32))
    mean = jnp.sum(squares, axis=1, keepdims=True) / model
    inv[...] = jnp.broadcast_to(lax.rsqrt(mean + EPS_NORM), inv.shape)

    col_copies = []

    for k in range(n_k):
        for o in range(n_f):
            normed = (x_ref[:, features(o, k)].astype(F32) * inv[:, :1]).astype(BF16)
            if o == 0:
                cols[k, 0] = normed
            else:
                nb[k, o - 1] = normed

    def send_columns(k):
        copies = []
        for o in range(1, n_f):
            at = n_f - o
            copies.append(
                send(nb.at[k, o - 1], cols.at[k, at], col_send.at[k, o - 1], col_recv.at[k, at - 1], f_peer(o))
            )
        col_copies.append(copies)

    half = width // 2
    bits = [1 << b for b in reversed(range(n_d.bit_length() - 1))]
    orders = [bits, bits[1::-1] + bits[2:]]
    pending = [first, []]

    def flip(mask):
        index = d
        for bit in bits:
            if mask & bit:
                index = index + bit * (1 - 2 * lax.rem(d // bit, 2))
        return index

    def spread(level):
        for copy in pending[0]:
            copy.wait_recv()
        pending[0] = []
        if level == len(bits):
            return
        for part, order in enumerate(orders):
            held = [0]
            for bit in order[:level]:
                held = held + [mask ^ bit for mask in held]
            bit = order[level]
            for mask in held:
                place = wall.at[flip(mask), :, :, pl.ds(part * half, half)]
                pending[0].append(
                    send(
                        place, place, hyp_send.at[part, (mask ^ bit) - 1], hyp_recv.at[part, (mask ^ bit) - 1],
                        (flip(bit), f),
                    )
                )

    def hat_gradient():
        def back_part(o, k):
            if o == 0:
                block = w_ref[k * chunk : (k + 1) * chunk]
            else:
                group = chunk // rows
                block = wall[k * group : (k + 1) * group, o - 1].reshape(chunk, width)
            back = dot_t(cot_ref[...], block)
            return (back * gain_all[o, :, k * chunk : (k + 1) * chunk]).astype(BF16)

        total = jnp.zeros((tok, 128), F32)
        for o in range(n_f):
            for k in range(n_k):
                hat = back_part(o, k)
                place = features(o, k)
                ig_ref[:, place] = hat
                term = hat.astype(F32) * (x_ref[:, place].astype(F32) * inv[:, :1])
                for at in range(0, chunk, 128):
                    total = total + term[:, at : at + 128]
        mean_term = jnp.sum(total, axis=1, keepdims=True) / model
        means[...] = jnp.broadcast_to(mean_term, means.shape)

    def finish(part):
        def step(at, carry):
            place = pl.ds(pl.multiple_of(at * 512, 512), 512)
            normed = x_ref[:, place].astype(F32) * inv[:, :1]
            hat32 = ig_ref[:, place].astype(F32)
            ig_ref[:, place] = (inv[:, :1] * (hat32 - normed * means[:, :1])).astype(BF16)
            return carry

        blocks = model // 512
        lax.fori_loop(part * blocks // 2, (part + 1) * blocks // 2, step, 0)

    slab_copies = []

    def gather_products(k):
        for copy in slab_copies[k]:
            copy.wait_recv()
        block = slabs[k].reshape(width, chunk)
        if k == 0:
            products[...] = dot_t(block, block)
        else:
            products[...] += dot_t(block, block)

    levels = len(bits)
    spread(0)
    send_columns(0)
    if n_k > 1:
        send_columns(1)
    spread(1)
    done = 1
    for copy in cot_copies + gain_copies:
        copy.wait_recv()
    cot_turned[...] = cot_all[...].reshape(n_f * tok, width).T
    for k in range(n_k):
        for copy in col_copies[k]:
            copy.wait_recv()
        if k + 2 < n_k:
            left(col_copies[k])
            send_columns(k + 2)
        place = slice(k * chunk, (k + 1) * chunk)
        cotangent = cot_all[...].reshape(n_f * tok, width)
        columns32 = cols[k].reshape(n_f * tok, chunk).astype(F32)
        scaled = (columns32 * gain_ref[:, place]).astype(BF16)
        grad = jnp.dot(cot_turned[...], scaled, preferred_element_type=F32)
        gsend[k] = (grad * scale).astype(BF16).reshape(n_d, slab, chunk)
        copies = []
        for o in range(1, n_d):
            copies.append(
                send(
                    gsend.at[k, lax.rem(d + o, n_d)], slabs.at[k, d],
                    slab_send.at[k, o - 1], slab_recv.at[k, n_d - o - 1], d_peer(o),
                )
            )
        slab_copies.append(copies)
        slabs[k, d] = gsend[k, d]
        back = dot_t(cotangent, w_ref[place])
        gain_grad = jnp.sum(back * columns32, axis=0, keepdims=True) * scale
        g_own[:, place] = gain_grad.astype(BF16).astype(F32)
        if 0 < k < n_k - 1 and done < levels:
            done += 1
            spread(done)
        if k:
            gather_products(k - 1)

    g_copies = []
    for o in range(1, n_d):
        g_copies.append(send(g_own, g_all.at[d], g_send.at[o - 1], g_recv.at[n_d - o - 1], d_peer(o)))
    g_all[d] = g_own[...]
    while done < levels:
        done += 1
        spread(done)
    hat_gradient()
    gather_products(n_k - 1)

    row = lax.broadcasted_iota(jnp.int32, (width, width), 0)
    lane = lax.broadcasted_iota(jnp.int32, (width, width), 1)
    same = lax.rem(row, slab) == lax.rem(lane, slab)
    by_row = jnp.sum(jnp.where(same, products[...], 0.0).reshape(n_d, slab, width), axis=1)
    column = lax.broadcasted_iota(jnp.int32, (n_d, 128), 1)
    gram_w = jnp.zeros((n_d, 128), F32)
    for s in range(n_d):
        part = jnp.sum(by_row[:, s * slab : (s + 1) * slab], axis=1, keepdims=True)
        gram_w = jnp.where(column == s, part, gram_w)
    gram1[d] = gram_w
    one_copies = []
    for o in range(1, n_d):
        one_copies.append(
            send(gram1.at[d], gram1.at[d], one_send.at[o - 1], one_recv.at[n_d - o - 1], d_peer(o))
        )
    finish(0)
    for copy in g_copies:
        copy.wait_recv()
    gains = g_all[...].reshape(n_d, owned)
    gram_g = jnp.zeros((n_d, 128), F32)
    for s in range(n_d):
        part = jnp.sum(gains * gains[s : s + 1], axis=1, keepdims=True)
        gram_g = jnp.where(column == s, part, gram_g)
    for copy in one_copies:
        copy.wait_recv()
    total = gram1[0]
    for s in range(1, n_d):
        total = total + gram1[s]
    gram2[f, 0] = total
    gram2[f, 1] = gram_g
    two_copies = []
    for o in range(1, n_f):
        two_copies.append(
            send(gram2.at[f], gram2.at[f], two_send.at[o - 1], two_recv.at[n_f - o - 1], f_peer(o))
        )
    finish(1)
    for copy in two_copies:
        copy.wait_recv()
    sum_w, sum_g = gram2[0, 0], gram2[0, 1]
    for s in range(1, n_f):
        sum_w = sum_w + gram2[s, 0]
        sum_g = sum_g + gram2[s, 1]
    coef_w, coef_g = coefficients(sum_w), coefficients(sum_g)
    gain_total = coef_g[0:1, 0:1] * gains[0:1]
    for s in range(1, n_d):
        gain_total = gain_total + coef_g[0:1, s : s + 1] * gains[s : s + 1]
    for at in range(owned // 128):
        gu_ref[at : at + 1] = gain_total[:, at * 128 : (at + 1) * 128]
    for k in range(n_k):
        weight_total = coef_w[0:1, 0:1] * slabs[k, 0].astype(F32)
        for s in range(1, n_d):
            weight_total = weight_total + coef_w[0:1, s : s + 1] * slabs[k, s].astype(F32)
        wu_ref[:, k * chunk : (k + 1) * chunk] = weight_total.astype(BF16)
    for copy in sent:
        copy.wait_send()


def body(n_d, n_f, layer_input, norm_gain, value_weight, value_cotangent):
    tok, model = layer_input.shape
    owned, width = value_weight.shape
    chunk = min(512, owned)
    n_k = owned // chunk
    rows, slab = owned // n_d, width // n_d
    dma = pltpu.SemaphoreType.DMA
    vmem = pl.BlockSpec(memory_space=pltpu.VMEM)
    pairs = [(n_f - 1,)] * 6 + [(n_k, n_f - 1)] * 2 + [(2, n_d - 1)] * 2 + [(n_k, n_d - 1)] * 2
    pairs += [(n_d - 1,)] * 4 + [(n_f - 1,)] * 2
    input_grad, weight, gain = pl.pallas_call(
        functools.partial(kernel, n_d, n_f, n_k),
        out_shape=(
            jax.ShapeDtypeStruct((tok, model), BF16),
            jax.ShapeDtypeStruct((slab, owned), BF16),
            jax.ShapeDtypeStruct((owned // 128, 128), F32),
        ),
        in_specs=[vmem] * 4,
        out_specs=(vmem,) * 3,
        scratch_shapes=[
            pltpu.VMEM((tok, 128), F32),
            pltpu.VMEM((tok, 128), F32),
            pltpu.VMEM((n_k, n_f - 1, tok, chunk), BF16),
            pltpu.VMEM((n_k, n_f, tok, chunk), BF16),
            pltpu.VMEM((n_f, tok, width), BF16),
            pltpu.VMEM((n_f, 1, owned), F32),
            pltpu.VMEM((n_d, n_f - 1, rows, width), BF16),
            pltpu.VMEM((n_k, n_d, slab, chunk), BF16),
            pltpu.VMEM((n_k, n_d, slab, chunk), BF16),
            pltpu.VMEM((width, n_f * tok), BF16),
            pltpu.VMEM((width, width), F32),
            pltpu.VMEM((1, owned), F32),
            pltpu.VMEM((n_d, 1, owned), F32),
            pltpu.VMEM((n_d, n_d, 128), F32),
            pltpu.VMEM((n_f, 2, n_d, 128), F32),
        ]
        + [dma(shape) for shape in pairs],
        compiler_params=pltpu.CompilerParams(
            collective_id=0, has_side_effects=True, vmem_limit_bytes=56 * 1024 * 1024
        ),
        cost_estimate=pl.CostEstimate(
            flops=8 * tok * model * width, bytes_accessed=8 * tok * model, transcendentals=0
        ),
    )(layer_input, norm_gain.reshape(1, owned), value_weight, value_cotangent)
    return (input_grad, weight.T, gain.reshape(owned).astype(BF16))


def solution(mesh):
    in_specs = (P(("dp", "fsdp"), None), P("fsdp"), P("fsdp", None), P(("dp", "fsdp"), None))
    out_specs = (P(("dp", "fsdp"), None), P("fsdp", "dp"), P("fsdp"))
    inner = functools.partial(body, mesh.shape["dp"], mesh.shape["fsdp"])
    return jax.shard_map(inner, mesh=mesh, in_specs=in_specs, out_specs=out_specs, check_vma=False)
```

```python
import functools
import math

import jax
import jax.numpy as jnp
from jax import lax
from jax.experimental import pallas as pl
from jax.experimental.pallas import tpu as pltpu
from jax.sharding import PartitionSpec as P

EPS_NORM = 1e-05
EPS_SUM = 1e-06
MESH = pl.DeviceIdType.MESH
F32 = jnp.float32
BF16 = jnp.bfloat16


def dot_t(a, b):
    return lax.dot_general(a, b, (((1,), (1,)), ((), ())), preferred_element_type=F32)


def coefficients(gram):
    count, lanes = gram.shape
    row = lax.broadcasted_iota(jnp.int32, gram.shape, 0)
    lane = lax.broadcasted_iota(jnp.int32, gram.shape, 1)
    coef = jnp.where(row == lane, 1.0, 0.0).astype(F32)
    stride = count // 2
    while stride:
        row_set = lax.rem(row // stride, 2) == 1
        lane_set = lax.rem(lane // stride, 2) == 1
        row_partner = jnp.where(row_set, row - stride, row + stride)

        def swap_rows(block):
            down = pltpu.roll(block, stride, 0)
            up = pltpu.roll(block, count - stride, 0)
            return jnp.where(row_set, down, up)

        def swap_lanes(block):
            down = pltpu.roll(block, stride, 1)
            up = pltpu.roll(block, lanes - stride, 1)
            return jnp.where(lane_set, down, up)

        own = jnp.where(row == lane, gram, 0.0)
        meet = jnp.where(row_partner == lane, gram, 0.0)

        def weights(axis):
            norm = jnp.maximum(jnp.sum(own, axis=axis, keepdims=True), 0.0)
            inner = jnp.sum(meet, axis=axis, keepdims=True)
            return jnp.broadcast_to(1.0 - inner / (2.0 * (norm + EPS_SUM)), gram.shape)

        mine, mine_lane = weights(1), weights(0)
        other, other_lane = swap_rows(mine), swap_lanes(mine_lane)
        coef = mine * coef + other * swap_rows(coef)
        gram = mine * gram + other * swap_rows(gram)
        gram = mine_lane * gram + other_lane * swap_lanes(gram)
        stride //= 2
    return coef


def kernel(
    n_d, n_f, n_k,
    x_ref, gain_ref, w_ref, cot_ref,
    ig_ref, wu_ref, gu_ref,
    inv, means, cot_plane, hat_out, hat_in, p_send, p_recv, h_send, h_recv, nb, cols, cot_all, gain_all, wall, gsend, slabs, cot_turned, products, g_own, g_all, gram1, gram2,
    w_send, w_recv, c_send, c_recv, n_send, n_recv, col_send, col_recv, hyp_send, hyp_recv,
    slab_send, slab_recv, g_send, g_recv, one_send, one_recv, two_send, two_recv,
):
    d, f = lax.axis_index("dp"), lax.axis_index("fsdp")
    tok, model = x_ref.shape
    owned, width = w_ref.shape
    chunk = owned // n_k
    rows = owned // n_d
    slab = width // n_d
    scale = 1.0 / math.sqrt(n_f * tok)
    direct = rows % 128 == 0
    sent = []

    def f_peer(o):
        return (d, lax.rem(f + o, n_f))

    def d_peer(o):
        return (lax.rem(d + o, n_d), f)

    def send(src, dst, send_sem, recv_sem, device):
        copy = pltpu.make_async_remote_copy(
            src_ref=src, dst_ref=dst, send_sem=send_sem, recv_sem=recv_sem,
            device_id=device, device_id_type=MESH,
        )
        copy.start()
        sent.append(copy)
        return copy

    def left(copies):
        for copy in copies:
            copy.wait_send()
        sent[:] = [copy for copy in sent if all(copy is not gone for gone in copies)]

    def features(o, k):
        return pl.ds(pl.multiple_of(lax.rem(f + o, n_f) * owned + k * chunk, 128), chunk)

    barrier = pltpu.get_barrier_semaphore()
    for o in range(1, n_f):
        pl.semaphore_signal(barrier, inc=1, device_id=f_peer(o), device_id_type=MESH)
    for o in range(1, n_d):
        pl.semaphore_signal(barrier, inc=1, device_id=d_peer(o), device_id_type=MESH)

    pl.semaphore_wait(barrier, n_f + n_d - 2)

    own_rows = pl.ds(pl.multiple_of(d * rows, 16), rows)
    first, cot_copies, gain_copies = [], [], []
    for o in range(1, n_f):
        at = n_f - o
        first.append(
            send(w_ref.at[own_rows], wall.at[d, at - 1], w_send.at[o - 1], w_recv.at[at - 1], f_peer(o))
        )
    for o in range(1, n_f):
        at = n_f - o
        cot_copies.append(
            send(cot_ref, cot_all.at[at], c_send.at[o - 1], c_recv.at[at - 1], f_peer(o))
        )
        gain_copies.append(
            send(gain_ref, gain_all.at[at], n_send.at[o - 1], n_recv.at[at - 1], f_peer(o))
        )
    plane_copies = []
    if direct:
        for o in range(1, n_d):
            plane_copies.append(
                send(cot_ref, cot_plane.at[d], p_send.at[o - 1], p_recv.at[n_d - o - 1], d_peer(o))
            )
        cot_plane[d] = cot_ref[...]
    cot_all[0] = cot_ref[...]
    gain_all[0] = gain_ref[...]

    def square(step, total):
        part = x_ref[:, pl.ds(pl.multiple_of(step * 512, 512), 512)].astype(F32)
        part = part * part
        for at in range(0, 512, 128):
            total = total + part[:, at : at + 128]
        return total

    squares = lax.fori_loop(0, model // 512, square, jnp.zeros((tok, 128), F32))
    mean = jnp.sum(squares, axis=1, keepdims=True) / model
    inv[...] = jnp.broadcast_to(lax.rsqrt(mean + EPS_NORM), inv.shape)

    col_copies = []

    for k in range(n_k):
        for o in range(n_f):
            normed = (x_ref[:, features(o, k)].astype(F32) * inv[:, :1]).astype(BF16)
            if o == 0:
                cols[k, 0] = normed
            else:
                nb[k, o - 1] = normed

    def send_columns(k):
        copies = []
        for o in range(1, n_f):
            at = n_f - o
            copies.append(
                send(nb.at[k, o - 1], cols.at[k, at], col_send.at[k, o - 1], col_recv.at[k, at - 1], f_peer(o))
            )
        col_copies.append(copies)

    half = width // 2
    bits = [1 << b for b in reversed(range(n_d.bit_length() - 1))]
    orders = [bits, bits[1::-1] + bits[2:]]
    pending = [first, []]

    def flip(mask):
        index = d
        for bit in bits:
            if mask & bit:
                index = index + bit * (1 - 2 * lax.rem(d // bit, 2))
        return index

    def spread(level):
        for copy in pending[0]:
            copy.wait_recv()
        pending[0] = []
        if level == len(bits):
            return
        for part, order in enumerate(orders):
            held = [0]
            for bit in order[:level]:
                held = held + [mask ^ bit for mask in held]
            bit = order[level]
            for mask in held:
                place = wall.at[flip(mask), :, :, pl.ds(part * half, half)]
                pending[0].append(
                    send(
                        place, place, hyp_send.at[part, (mask ^ bit) - 1], hyp_recv.at[part, (mask ^ bit) - 1],
                        (flip(bit), f),
                    )
                )

    hat_copies = []

    def send_hats():
        for copy in plane_copies:
            copy.wait_recv()
        tokens = cot_plane[...].reshape(n_d * tok, width)
        for o in range(n_f):
            block = w_ref[own_rows] if o == 0 else wall[d, o - 1]
            own_gain = gain_all[o, :, pl.ds(pl.multiple_of(d * rows, 128), rows)]
            hat = (dot_t(tokens, block) * own_gain).astype(BF16)
            hat_out[:, o] = hat.reshape(n_d, tok, rows)
        for o in range(1, n_d):
            hat_copies.append(
                send(
                    hat_out.at[lax.rem(d + o, n_d)], hat_in.at[d], h_send.at[o - 1], h_recv.at[n_d - o - 1], d_peer(o),
                )
            )
        hat_in[d] = hat_out[d]

    def place_hats():
        for copy in hat_copies:
            copy.wait_recv()
        total = jnp.zeros((tok, 128), F32)
        for s in range(n_d):
            for o in range(n_f):
                place = pl.ds(pl.multiple_of(lax.rem(f + o, n_f) * owned + s * rows, 128), rows)
                hat = hat_in[s, o]
                ig_ref[:, place] = hat
                term = hat.astype(F32) * (x_ref[:, place].astype(F32) * inv[:, :1])
                for at in range(0, rows, 128):
                    total = total + term[:, at : at + 128]
        means[...] = jnp.broadcast_to(jnp.sum(total, axis=1, keepdims=True) / model, means.shape)

    def hat_gradient():
        def back_part(o, k):
            if o == 0:
                block = w_ref[k * chunk : (k + 1) * chunk]
            else:
                group = chunk // rows
                block = wall[k * group : (k + 1) * group, o - 1].reshape(chunk, width)
            back = dot_t(cot_ref[...], block)
            return (back * gain_all[o, :, k * chunk : (k + 1) * chunk]).astype(BF16)

        total = jnp.zeros((tok, 128), F32)
        for o in range(n_f):
            for k in range(n_k):
                hat = back_part(o, k)
                place = features(o, k)
                ig_ref[:, place] = hat
                term = hat.astype(F32) * (x_ref[:, place].astype(F32) * inv[:, :1])
                for at in range(0, chunk, 128):
                    total = total + term[:, at : at + 128]
        mean_term = jnp.sum(total, axis=1, keepdims=True) / model
        means[...] = jnp.broadcast_to(mean_term, means.shape)

    def finish(part):
        def step(at, carry):
            place = pl.ds(pl.multiple_of(at * 512, 512), 512)
            normed = x_ref[:, place].astype(F32) * inv[:, :1]
            hat32 = ig_ref[:, place].astype(F32)
            ig_ref[:, place] = (inv[:, :1] * (hat32 - normed * means[:, :1])).astype(BF16)
            return carry

        blocks = model // 512
        lax.fori_loop(part * blocks // 2, (part + 1) * blocks // 2, step, 0)

    slab_copies = []

    def gather_products(k):
        for copy in slab_copies[k]:
            copy.wait_recv()
        block = slabs[k].reshape(width, chunk)
        if k == 0:
            products[...] = dot_t(block, block)
        else:
            products[...] += dot_t(block, block)

    levels = len(bits)
    if direct:
        send_columns(0)
        for copy in first + gain_copies:
            copy.wait_recv()
        if n_k > 1:
            send_columns(1)
        send_hats()
        done = levels
    else:
        spread(0)
        send_columns(0)
        if n_k > 1:
            send_columns(1)
        spread(1)
        done = 1
        for copy in gain_copies:
            copy.wait_recv()
    for copy in cot_copies:
        copy.wait_recv()
    cot_turned[...] = cot_all[...].reshape(n_f * tok, width).T
    for k in range(n_k):
        for copy in col_copies[k]:
            copy.wait_recv()
        if k + 2 < n_k:
            left(col_copies[k])
            send_columns(k + 2)
        place = slice(k * chunk, (k + 1) * chunk)
        cotangent = cot_all[...].reshape(n_f * tok, width)
        columns32 = cols[k].reshape(n_f * tok, chunk).astype(F32)
        scaled = (columns32 * gain_ref[:, place]).astype(BF16)
        grad = jnp.dot(cot_turned[...], scaled, preferred_element_type=F32)
        gsend[k] = (grad * scale).astype(BF16).reshape(n_d, slab, chunk)
        copies = []
        for o in range(1, n_d):
            copies.append(
                send(
                    gsend.at[k, lax.rem(d + o, n_d)], slabs.at[k, d],
                    slab_send.at[k, o - 1], slab_recv.at[k, n_d - o - 1], d_peer(o),
                )
            )
        slab_copies.append(copies)
        slabs[k, d] = gsend[k, d]
        back = dot_t(cotangent, w_ref[place])
        gain_grad = jnp.sum(back * columns32, axis=0, keepdims=True) * scale
        g_own[:, place] = gain_grad.astype(BF16).astype(F32)
        if 0 < k < n_k - 1 and done < levels:
            done += 1
            spread(done)
        if k:
            gather_products(k - 1)

    g_copies = []
    for o in range(1, n_d):
        g_copies.append(send(g_own, g_all.at[d], g_send.at[o - 1], g_recv.at[n_d - o - 1], d_peer(o)))
    g_all[d] = g_own[...]
    while done < levels:
        done += 1
        spread(done)
    place_hats() if direct else hat_gradient()
    gather_products(n_k - 1)

    row = lax.broadcasted_iota(jnp.int32, (width, width), 0)
    lane = lax.broadcasted_iota(jnp.int32, (width, width), 1)
    same = lax.rem(row, slab) == lax.rem(lane, slab)
    by_row = jnp.sum(jnp.where(same, products[...], 0.0).reshape(n_d, slab, width), axis=1)
    column = lax.broadcasted_iota(jnp.int32, (n_d, 128), 1)
    gram_w = jnp.zeros((n_d, 128), F32)
    for s in range(n_d):
        part = jnp.sum(by_row[:, s * slab : (s + 1) * slab], axis=1, keepdims=True)
        gram_w = jnp.where(column == s, part, gram_w)
    gram1[d] = gram_w
    one_copies = []
    for o in range(1, n_d):
        one_copies.append(
            send(gram1.at[d], gram1.at[d], one_send.at[o - 1], one_recv.at[n_d - o - 1], d_peer(o))
        )
    finish(0)
    for copy in g_copies:
        copy.wait_recv()
    gains = g_all[...].reshape(n_d, owned)
    gram_g = jnp.zeros((n_d, 128), F32)
    for s in range(n_d):
        part = jnp.sum(gains * gains[s : s + 1], axis=1, keepdims=True)
        gram_g = jnp.where(column == s, part, gram_g)
    for copy in one_copies:
        copy.wait_recv()
    total = gram1[0]
    for s in range(1, n_d):
        total = total + gram1[s]
    gram2[f, 0] = total
    gram2[f, 1] = gram_g
    two_copies = []
    for o in range(1, n_f):
        two_copies.append(
            send(gram2.at[f], gram2.at[f], two_send.at[o - 1], two_recv.at[n_f - o - 1], f_peer(o))
        )
    finish(1)
    for copy in two_copies:
        copy.wait_recv()
    sum_w, sum_g = gram2[0, 0], gram2[0, 1]
    for s in range(1, n_f):
        sum_w = sum_w + gram2[s, 0]
        sum_g = sum_g + gram2[s, 1]
    coef_w, coef_g = coefficients(sum_w), coefficients(sum_g)
    gain_total = coef_g[0:1, 0:1] * gains[0:1]
    for s in range(1, n_d):
        gain_total = gain_total + coef_g[0:1, s : s + 1] * gains[s : s + 1]
    for at in range(owned // 128):
        gu_ref[at : at + 1] = gain_total[:, at * 128 : (at + 1) * 128]
    for k in range(n_k):
        weight_total = coef_w[0:1, 0:1] * slabs[k, 0].astype(F32)
        for s in range(1, n_d):
            weight_total = weight_total + coef_w[0:1, s : s + 1] * slabs[k, s].astype(F32)
        wu_ref[:, k * chunk : (k + 1) * chunk] = weight_total.astype(BF16)
    for copy in sent:
        copy.wait_send()


def body(n_d, n_f, layer_input, norm_gain, value_weight, value_cotangent):
    tok, model = layer_input.shape
    owned, width = value_weight.shape
    chunk = min(512, owned)
    n_k = owned // chunk
    rows, slab = owned // n_d, width // n_d
    dma = pltpu.SemaphoreType.DMA
    hat_shape = (n_d, n_f, tok, rows) if rows % 128 == 0 else (1, 1, 16, 128)
    vmem = pl.BlockSpec(memory_space=pltpu.VMEM)
    pairs = [(n_f - 1,)] * 6 + [(n_k, n_f - 1)] * 2 + [(2, n_d - 1)] * 2 + [(n_k, n_d - 1)] * 2
    pairs += [(n_d - 1,)] * 4 + [(n_f - 1,)] * 2
    input_grad, weight, gain = pl.pallas_call(
        functools.partial(kernel, n_d, n_f, n_k),
        out_shape=(
            jax.ShapeDtypeStruct((tok, model), BF16),
            jax.ShapeDtypeStruct((slab, owned), BF16),
            jax.ShapeDtypeStruct((owned // 128, 128), F32),
        ),
        in_specs=[vmem] * 4,
        out_specs=(vmem,) * 3,
        scratch_shapes=[
            pltpu.VMEM((tok, 128), F32),
            pltpu.VMEM((tok, 128), F32),
            pltpu.VMEM((n_d, tok, width), BF16),
            pltpu.VMEM(hat_shape, BF16),
            pltpu.VMEM(hat_shape, BF16),
            *[dma((n_d - 1,))] * 4,
            pltpu.VMEM((n_k, n_f - 1, tok, chunk), BF16),
            pltpu.VMEM((n_k, n_f, tok, chunk), BF16),
            pltpu.VMEM((n_f, tok, width), BF16),
            pltpu.VMEM((n_f, 1, owned), F32),
            pltpu.VMEM((n_d, n_f - 1, rows, width), BF16),
            pltpu.VMEM((n_k, n_d, slab, chunk), BF16),
            pltpu.VMEM((n_k, n_d, slab, chunk), BF16),
            pltpu.VMEM((width, n_f * tok), BF16),
            pltpu.VMEM((width, width), F32),
            pltpu.VMEM((1, owned), F32),
            pltpu.VMEM((n_d, 1, owned), F32),
            pltpu.VMEM((n_d, n_d, 128), F32),
            pltpu.VMEM((n_f, 2, n_d, 128), F32),
        ]
        + [dma(shape) for shape in pairs],
        compiler_params=pltpu.CompilerParams(
            collective_id=0, has_side_effects=True, vmem_limit_bytes=56 * 1024 * 1024
        ),
        cost_estimate=pl.CostEstimate(
            flops=8 * tok * model * width, bytes_accessed=8 * tok * model, transcendentals=0
        ),
    )(layer_input, norm_gain.reshape(1, owned), value_weight, value_cotangent)
    return (input_grad, weight.T, gain.reshape(owned).astype(BF16))


def solution(mesh):
    in_specs = (P(("dp", "fsdp"), None), P("fsdp"), P("fsdp", None), P(("dp", "fsdp"), None))
    out_specs = (P(("dp", "fsdp"), None), P("fsdp", "dp"), P("fsdp"))
    inner = functools.partial(body, mesh.shape["dp"], mesh.shape["fsdp"])
    return jax.shard_map(inner, mesh=mesh, in_specs=in_specs, out_specs=out_specs, check_vma=False)
```
